32 devices in a mesh: rep: 2 (over x), gx: 8 (over z, y), yz: 2 (over core).
Axes of the slice: x: 2, y: 2, z: 4, core: 2. Of those that a mesh axis runs over, the one named last changes fastest.
Arguments:
- hidden: bfloat16 [2, 32, 16384], P(None, 'rep', 'gx'), parts along dimension 1, may hold values from -80 to 80
- norm_gain: float32 [16384], P('gx'), may hold values from 0.5 to 1.5
- query_weight: bfloat16 [16384, 8192], P('gx', 'yz'), may hold values from -0.046875 to 0.046875
- key_matrix: bfloat16 [16384, 512], P('gx', 'yz'), may hold values from -0.046875 to 0.046875
- value_matrix: bfloat16 [16384, 512], P('gx', 'yz'), may hold values from -0.046875 to 0.046875
- output_weight: bfloat16 [8192, 16384], P('yz', 'gx'), may hold values from -0.0625 to 0.0625
- key_cache_rows: bfloat16 [32, 2048, 512], P(('rep', 'gx', 'yz')), parts along dimension 0, may hold values from -2500 to 2500
- value_cache_rows: bfloat16 [32, 2048, 512], P(('rep', 'gx', 'yz')), parts along dimension 0, may hold values from -6 to 6
- lengths: int32 [32], P(('rep', 'gx', 'yz')), parts along dimension 0, may hold values from 2 to 2046, as said below
- positions: int32 [32], P('rep'), parts along dimension 0, may hold values from 0 to 1023
Outputs:
- out: bfloat16 [2, 32, 16384], P(None, 'rep', 'gx'), parts along dimension 1
- new_keys: bfloat16 [2, 32, 512], P(None, ('rep', 'gx', 'yz')), parts along dimension 1
- new_values: bfloat16 [2, 32, 512], P(None, ('rep', 'gx', 'yz')), parts along dimension 1
The draws below stay inside these ranges and needn't reach their ends.
There are 2 independent parts, one for each index of `rep`. The reference program is written for one: setup_inputs(seed, part) draws one part's arguments, and reference() takes and returns one part's arrays. A program takes and returns all parts, laid end to end along the dimension named above; an argument that names none is the same for every part. Nothing has to cross between parts.
Inputs may be any that keep to these rules, and one draw needn't show every extreme that they name: Row r has lengths[r] valid cached entries at cache slots 0 to lengths[r] - 1; some row holds 2046.
All inputs are finite; a program needn't handle non-finite values.
Results may differ from the reference program's by a relative error of at most 0.0051.
Values may be sent and summed in bfloat16 or wider, within the bound.
A program may use at most 128 MiB of HBM per device.

```python
import jax
import jax.numpy as jnp
from jax import lax

MODEL_WIDTH = 16384
QUERY_HEADS = 64
KEY_VALUE_HEADS = 4
HEAD_SIZE = 128
STEPS = 2
CONTEXT_SLOTS = 2048
REPLICA_ROWS = 16


def draw_hidden(key, part):
    key = jax.random.fold_in(key, 1)
    initial_key, second_key = jax.random.split(key, 2)
    column = jnp.arange(MODEL_WIDTH, dtype=jnp.float32) / MODEL_WIDTH
    rough = jnp.exp(jax.random.uniform(second_key, (MODEL_WIDTH,), minval=-0.7, maxval=0.7))
    scales = 0.6 * 3.0 ** column * rough
    rotary_base = jnp.clip(jax.random.normal(initial_key, (STEPS, REPLICA_ROWS, MODEL_WIDTH)), -6.0, 6.0)
    return (rotary_base * scales).astype(jnp.bfloat16)


def draw_key_cache_rows(key, part):
    key = jax.random.fold_in(key, 2)
    initial_key = jax.random.fold_in(key, 0)
    rotary_base = jnp.clip(jax.random.normal(initial_key, (REPLICA_ROWS, CONTEXT_SLOTS, KEY_VALUE_HEADS * HEAD_SIZE)), -6.0, 6.0)
    return rotary_base.astype(jnp.bfloat16)


def draw_lengths(key, part):
    key = jax.random.fold_in(key, 3)
    initial_key, second_key = jax.random.split(key, 2)
    drawn = jax.random.randint(initial_key, (REPLICA_ROWS,), 2, CONTEXT_SLOTS - 1)
    chosen = jax.random.randint(second_key, (), 0, REPLICA_ROWS)
    return jnp.where(jnp.arange(REPLICA_ROWS) == chosen, CONTEXT_SLOTS - 2, drawn).astype(jnp.int32)


def plant(result, own_key, smallest, high):
    longest = result.shape.index(max(result.shape))
    spots = []
    for shift in (0, 1):
        where = [jax.random.randint(jax.random.fold_in(own_key, axis), (), 0, length) for axis, length in enumerate(result.shape)]
        where[longest] = (where[longest] + shift) % result.shape[longest]
        spots.append(tuple(where))
    return result.at[spots[0]].set(smallest).at[spots[1]].set(high)


def level_of(key, extent, shards, smallest, largest):
    def one(axis_at, parts):
        draws = jax.random.uniform(jax.random.fold_in(jax.random.fold_in(key, 6), axis_at), (parts,), jnp.float32, smallest / len(shards), largest / len(shards))
        return jnp.repeat(jnp.exp(draws), extent[axis_at] // parts).reshape((-1,) + (1,) * (len(extent) - axis_at - 1))

    level = one(*shards[0])
    for cut in shards[1:]:
        level = level * one(*cut)
    return level


def noise(rng, dims, deviation, most, shards=(), held_as=jnp.bfloat16):
    loudness = level_of(rng, dims, shards, -0.22, 0.18) if shards else 1.0
    entries = jax.random.normal(rng, dims, jnp.float32) * deviation * loudness
    return jnp.minimum(jnp.maximum(entries, -most), most).astype(held_as)


def setup_inputs(seed: int = 0, part: int = 0) -> dict:
    seeds = jax.random.split(jax.random.key(seed), 11)
    part_splits = jax.random.split(jax.random.fold_in(seeds[10], part), 11)
    hidden = draw_hidden(jax.random.fold_in(jax.random.fold_in(seeds[10], part), 71), part)
    norm_gain = jnp.clip(1.0 + 0.1 * jax.random.normal(seeds[1], (MODEL_WIDTH,), jnp.float32), 0.5, 1.5)
    query_weight = noise(seeds[2], (MODEL_WIDTH, QUERY_HEADS * HEAD_SIZE), MODEL_WIDTH ** -0.5, 0.046875, ((0, 8), (1, 2)))
    key_matrix = noise(seeds[3], (MODEL_WIDTH, KEY_VALUE_HEADS * HEAD_SIZE), MODEL_WIDTH ** -0.5, 0.046875, ((0, 8), (1, 2)))
    value_matrix = noise(seeds[4], (MODEL_WIDTH, KEY_VALUE_HEADS * HEAD_SIZE), MODEL_WIDTH ** -0.5, 0.046875, ((0, 8), (1, 2)))
    output_weight = noise(seeds[5], (QUERY_HEADS * HEAD_SIZE, MODEL_WIDTH), (QUERY_HEADS * HEAD_SIZE) ** -0.5, 0.0625, ((0, 2), (1, 8)))
    key_cache_rows = draw_key_cache_rows(jax.random.fold_in(jax.random.fold_in(seeds[10], part), 71), part)
    value_cache_rows = noise(part_splits[7], (REPLICA_ROWS, CONTEXT_SLOTS, KEY_VALUE_HEADS * HEAD_SIZE), 1.0, 6.0, ((0, 16),))
    lengths = draw_lengths(jax.random.fold_in(jax.random.fold_in(seeds[10], part), 71), part)
    positions = plant(jax.random.randint(part_splits[9], (REPLICA_ROWS,), 0, 1024), jax.random.fold_in(part_splits[9], 1), 0, 1023).astype(jnp.int32)
    return {"hidden": hidden, "norm_gain": norm_gain, "query_weight": query_weight, "key_matrix": key_matrix, "value_matrix": value_matrix, "output_weight": output_weight, "key_cache_rows": key_cache_rows, "value_cache_rows": value_cache_rows, "lengths": lengths, "positions": positions}


def rotate(values, offsets):
    half = HEAD_SIZE // 2
    filled_count = values.shape[0]
    heads = values.shape[1] // HEAD_SIZE
    freq = 500000.0 ** (-2.0 * jnp.arange(half, dtype=jnp.float32) / HEAD_SIZE)
    angles = offsets.astype(jnp.float32)[:, None] * freq[None, :]
    cosine = jnp.cos(angles)[:, None, :]
    sine = jnp.sin(angles)[:, None, :]
    split = values.reshape(filled_count, heads, HEAD_SIZE)
    first = split[:, :, :half]
    second = split[:, :, half:]
    joined = jnp.concatenate([first * cosine - second * sine, second * cosine + first * sine], axis=2)
    return joined.reshape(filled_count, heads * HEAD_SIZE)

def reference(hidden, norm_gain, query_weight, key_matrix, value_matrix, output_weight, key_cache_rows, value_cache_rows, lengths, positions):
    group_size = QUERY_HEADS // KEY_VALUE_HEADS
    scale = HEAD_SIZE ** (-0.5)
    batch_rows = hidden.shape[1]
    every_key = key_cache_rows.astype(jnp.float32).reshape(batch_rows, CONTEXT_SLOTS, KEY_VALUE_HEADS, HEAD_SIZE)
    every_value = value_cache_rows.astype(jnp.float32).reshape(batch_rows, CONTEXT_SLOTS, KEY_VALUE_HEADS, HEAD_SIZE)
    valid = jnp.arange(CONTEXT_SLOTS)[None, :] < lengths[:, None]
    latest_keys = []
    latest_values = []
    outputs = []
    for decode_step in range(STEPS):
        inputs = hidden[decode_step].astype(jnp.float32)
        inverse = lax.rsqrt(lax.optimization_barrier(jnp.mean(inputs * inputs, axis=1, keepdims=True)) + 1e-05)
        scaled = (inputs * norm_gain[None, :]).astype(jnp.bfloat16)
        query = jnp.dot(scaled, query_weight, preferred_element_type=jnp.float32) * inverse
        keyed = jnp.dot(scaled, key_matrix, preferred_element_type=jnp.float32) * inverse
        valued = jnp.dot(scaled, value_matrix, preferred_element_type=jnp.float32) * inverse
        offsets = positions + decode_step
        turned_query = rotate(query, offsets).astype(jnp.bfloat16)
        latest_keys.append(rotate(keyed, offsets).astype(jnp.bfloat16))
        latest_values.append(valued.astype(jnp.bfloat16))
        grouped_queries = lax.optimization_barrier(turned_query).astype(jnp.float32).reshape(batch_rows, KEY_VALUE_HEADS, group_size, HEAD_SIZE)
        cached_scores = jnp.einsum('bhgd,bphd->bhgp', grouped_queries, every_key) * scale
        cached_scores = jnp.where(valid[:, None, None, :], cached_scores, -jnp.inf)
        newest_key_block = jnp.stack(latest_keys).astype(jnp.float32).reshape(decode_step + 1, batch_rows, KEY_VALUE_HEADS, HEAD_SIZE)
        newest_value_block = jnp.stack(latest_values).astype(jnp.float32).reshape(decode_step + 1, batch_rows, KEY_VALUE_HEADS, HEAD_SIZE)
        recent_scores = jnp.einsum('bhgd,nbhd->bhgn', grouped_queries, newest_key_block) * scale
        highest = jnp.maximum(lax.optimization_barrier(jnp.max(cached_scores, axis=3, keepdims=True)), lax.optimization_barrier(jnp.max(recent_scores, axis=3, keepdims=True)))
        cached_w = jnp.exp(cached_scores - highest)
        recent_w = jnp.exp(recent_scores - highest)
        total = lax.optimization_barrier(jnp.sum(cached_w, axis=3)) + lax.optimization_barrier(jnp.sum(recent_w, axis=3))
        cached_r = lax.optimization_barrier(cached_w.astype(jnp.bfloat16)).astype(jnp.float32)
        recent_r = lax.optimization_barrier(recent_w.astype(jnp.bfloat16)).astype(jnp.float32)
        weighted = jnp.einsum('bhgp,bphd->bhgd', cached_r, every_value) + jnp.einsum('bhgn,nbhd->bhgd', recent_r, newest_value_block)
        attended = (weighted / total[..., None]).astype(jnp.bfloat16).reshape(batch_rows, QUERY_HEADS * HEAD_SIZE)
        mixed = inputs + jnp.dot(attended, output_weight, preferred_element_type=jnp.float32)
        outputs.append(mixed.astype(jnp.bfloat16))
    return (jnp.stack(outputs), jnp.stack(latest_keys), jnp.stack(latest_values))
```

```python
import jax
import jax.numpy as jnp
from jax import lax
from jax.sharding import PartitionSpec as P

MODEL_WIDTH = 16384
QUERY_HEADS = 64
KEY_VALUE_HEADS = 4
HEAD_SIZE = 128
STEPS = 2
CONTEXT_SLOTS = 2048


def rotate(values, offsets):
    half = HEAD_SIZE // 2
    filled_count = values.shape[0]
    heads = values.shape[1] // HEAD_SIZE
    freq = 500000.0 ** (-2.0 * jnp.arange(half, dtype=jnp.float32) / HEAD_SIZE)
    angles = offsets.astype(jnp.float32)[:, None] * freq[None, :]
    cosine = jnp.cos(angles)[:, None, :]
    sine = jnp.sin(angles)[:, None, :]
    split = values.reshape(filled_count, heads, HEAD_SIZE)
    first = split[:, :, :half]
    second = split[:, :, half:]
    joined = jnp.concatenate(
        [first * cosine - second * sine, second * cosine + first * sine], axis=2
    )
    return joined.reshape(filled_count, heads * HEAD_SIZE)


def attend(queries, row_keys, row_values, newest_keys, newest_values, length):
    group_size = QUERY_HEADS // KEY_VALUE_HEADS
    scale = HEAD_SIZE ** (-0.5)
    grouped = queries.reshape(STEPS, KEY_VALUE_HEADS, group_size, HEAD_SIZE)
    grouped = grouped.transpose(1, 0, 2, 3).reshape(
        KEY_VALUE_HEADS, STEPS * group_size, HEAD_SIZE
    )
    valid = jnp.arange(CONTEXT_SLOTS) < length
    query_step = jnp.arange(STEPS * group_size) // group_size
    seen = jnp.arange(STEPS)[None, :] <= query_step[:, None]
    results = []
    for head in range(KEY_VALUE_HEADS):
        part = slice(head * HEAD_SIZE, (head + 1) * HEAD_SIZE)
        own = grouped[head]
        cached = scale * lax.dot_general(
            own, row_keys[:, part], (((1,), (1,)), ((), ())), preferred_element_type=jnp.float32
        )
        recent = scale * lax.dot_general(
            own, newest_keys[:, part], (((1,), (1,)), ((), ())), preferred_element_type=jnp.float32
        )
        cached = jnp.where(valid[None, :], cached, -jnp.inf)
        recent = jnp.where(seen, recent, -jnp.inf)
        highest = jnp.maximum(
            jnp.max(cached, axis=1, keepdims=True), jnp.max(recent, axis=1, keepdims=True)
        )
        cached_w = jnp.exp(cached - highest)
        recent_w = jnp.exp(recent - highest)
        total = jnp.sum(cached_w, axis=1) + jnp.sum(recent_w, axis=1)
        weighted = jnp.dot(
            cached_w.astype(jnp.bfloat16), row_values[:, part], preferred_element_type=jnp.float32
        ) + jnp.dot(
            recent_w.astype(jnp.bfloat16),
            newest_values[:, part],
            preferred_element_type=jnp.float32,
        )
        results.append((weighted / total[:, None]).astype(jnp.bfloat16))
    joined = jnp.stack(results).reshape(KEY_VALUE_HEADS, STEPS, group_size, HEAD_SIZE)
    return joined.transpose(1, 0, 2, 3).reshape(STEPS, QUERY_HEADS * HEAD_SIZE)


def per_device(
    hidden,
    norm_gain,
    query_weight,
    key_matrix,
    value_matrix,
    output_weight,
    key_cache_rows,
    value_cache_rows,
    lengths,
    positions,
):
    batch_rows = hidden.shape[1]
    width = hidden.shape[2]
    share = batch_rows // lax.axis_size("gx")
    first_row = lax.axis_index("gx") * share
    query_cols = query_weight.shape[1]
    key_cols = key_matrix.shape[1]
    own_positions = lax.dynamic_slice_in_dim(positions, first_row, share, 0)
    inputs = hidden.transpose(1, 0, 2).reshape(batch_rows * STEPS, width).astype(jnp.float32)
    squares = jnp.sum(inputs * inputs, axis=1, keepdims=True)
    scaled = (inputs * norm_gain[None, :]).astype(jnp.bfloat16)
    sums = jnp.concatenate(
        [
            jnp.dot(scaled, query_weight, preferred_element_type=jnp.float32),
            jnp.dot(scaled, key_matrix, preferred_element_type=jnp.float32),
            jnp.dot(scaled, value_matrix, preferred_element_type=jnp.float32),
            jnp.broadcast_to(squares, (batch_rows * STEPS, HEAD_SIZE)),
        ],
        axis=1,
    )
    own = lax.psum_scatter(sums, "gx", scatter_dimension=0, tiled=True)
    cols = query_cols + 2 * key_cols
    inverse = lax.rsqrt(own[:, cols : cols + 1] / MODEL_WIDTH + 1e-05)
    projected = own[:, :cols] * inverse
    offsets = (own_positions[:, None] + jnp.arange(STEPS)[None, :]).reshape(share * STEPS)
    turned = rotate(projected[:, : query_cols + key_cols], offsets).astype(jnp.bfloat16)
    new_value = projected[:, query_cols + key_cols :].astype(jnp.bfloat16)
    packed = jnp.concatenate([turned, new_value], axis=1)
    halves = lax.axis_size("yz")
    swapped = lax.all_to_all(
        packed.reshape(halves, STEPS, cols), "yz", split_axis=0, concat_axis=0, tiled=True
    )
    swapped = swapped.transpose(1, 0, 2)
    row_query = swapped[:, :, :query_cols].reshape(STEPS, halves * query_cols)
    row_key = swapped[:, :, query_cols : query_cols + key_cols].reshape(STEPS, halves * key_cols)
    row_value = swapped[:, :, query_cols + key_cols :].reshape(STEPS, halves * key_cols)
    attended = attend(
        row_query, key_cache_rows[0], value_cache_rows[0], row_key, row_value, lengths[0]
    )
    head_pair = lax.all_to_all(attended, "yz", split_axis=1, concat_axis=0, tiled=True)
    gathered = lax.all_gather(head_pair, "gx", axis=0, tiled=True)
    partial_out = jnp.dot(gathered, output_weight, preferred_element_type=jnp.float32)
    mixed = inputs + lax.psum(partial_out.astype(jnp.bfloat16), "yz").astype(jnp.float32)
    out = mixed.astype(jnp.bfloat16).reshape(batch_rows, STEPS, width).transpose(1, 0, 2)
    return (out, row_key[:, None, :], row_value[:, None, :])


def solution(mesh):
    in_specs = (
        P(None, "rep", "gx"),
        P("gx"),
        P("gx", "yz"),
        P("gx", "yz"),
        P("gx", "yz"),
        P("yz", "gx"),
        P(("rep", "gx", "yz"), None, None),
        P(("rep", "gx", "yz"), None, None),
        P(("rep", "gx", "yz")),
        P("rep"),
    )
    out_specs = (
        P(None, "rep", "gx"),
        P(None, ("rep", "gx", "yz"), None),
        P(None, ("rep", "gx", "yz"), None),
    )
    return jax.shard_map(
        per_device, mesh=mesh, in_specs=in_specs, out_specs=out_specs, check_vma=False
    )
```

```python
import functools

import jax
import jax.numpy as jnp
from jax import lax
from jax.experimental import pallas as pl
from jax.experimental.pallas import tpu as pltpu
from jax.sharding import PartitionSpec as P

MODEL_WIDTH = 16384
HEAD_SIZE = 128
STEPS = 2
GROUP = 16
CHUNK = 512
OUT_PARTS = 4
MESH = pl.DeviceIdType.MESH


def remote(src, dst, send_sem, recv_sem, device):
    return pltpu.make_async_remote_copy(
        src_ref=src,
        dst_ref=dst,
        send_sem=send_sem,
        recv_sem=recv_sem,
        device_id=device,
        device_id_type=MESH,
    )


def kernel(
    n,
    rows_ref,
    x_ref,
    gain_ref,
    freq_ref,
    lengths_ref,
    positions_ref,
    qw_hbm,
    kw_hbm,
    vw_hbm,
    ow_hbm,
    kc_hbm,
    vc_hbm,
    out_ref,
    newk_ref,
    newv_ref,
    weights,
    kc,
    vc,
    ow,
    scaled,
    part,
    recv,
    sq_part,
    sq_recv,
    turned,
    q_send,
    q_all,
    att,
    gathered,
    wide,
    lhs,
    p_send,
    p_recv,
    w_sem,
    c_sem,
    o_sem,
    rs_send,
    rs_recv,
    sq_ssem,
    sq_rsem,
    q_ssem,
    q_rsem,
    g_ssem,
    g_rsem,
    p_ssem,
    p_rsem,
):
    me = lax.axis_index("gx")
    core = lax.axis_index("yz")
    other = 1 - core
    flat = me * 2 + core
    chunks = weights.shape[0]
    q_chunks = chunks - 1
    key_cols = kw_hbm.shape[1]
    out_cols = ow.shape[2]
    every = 2 * n

    for c in range(q_chunks):
        pltpu.make_async_copy(
            qw_hbm.at[:, c * CHUNK : (c + 1) * CHUNK], weights.at[c], w_sem.at[c]
        ).start()
    last = weights.at[q_chunks]
    pltpu.make_async_copy(kw_hbm, last.at[:, :key_cols], w_sem.at[q_chunks]).start()
    pltpu.make_async_copy(vw_hbm, last.at[:, key_cols:], w_sem.at[q_chunks]).start()
    pltpu.make_async_copy(kc_hbm, kc, c_sem.at[0]).start()
    pltpu.make_async_copy(vc_hbm, vc, c_sem.at[1]).start()
    for c in range(OUT_PARTS):
        pltpu.make_async_copy(
            ow_hbm.at[:, c * out_cols : (c + 1) * out_cols], ow.at[c], o_sem.at[c]
        ).start()

    barrier = pltpu.get_barrier_semaphore()

    def greet(t, carry):
        target = lax.rem(flat + t, every)
        pl.semaphore_signal(
            barrier,
            inc=1,
            device_id={"gx": target // 2, "yz": lax.rem(target, 2)},
            device_id_type=MESH,
        )
        return carry

    lax.fori_loop(1, every, greet, 0)

    xf = rows_ref[...].astype(jnp.float32)
    squares = jnp.sum(xf * xf, axis=1, keepdims=True)
    squares = jnp.broadcast_to(squares, (squares.shape[0], HEAD_SIZE))
    scaled[...] = (xf * gain_ref[...]).astype(jnp.bfloat16)
    for g in range(n):
        sq_part[g] = squares[4 * g : 4 * g + 4]
    turned[...] = jnp.zeros_like(turned)

    pl.semaphore_wait(barrier, every - 1)

    def sq_copy(d):
        target = lax.rem(me + d, n)
        return remote(
            sq_part.at[target], sq_recv.at[me], sq_ssem.at[d], sq_rsem.at[d], {"gx": target}
        )

    def rs_copy(d, c):
        target = lax.rem(me + d, n)
        return remote(
            part.at[target, c], recv.at[me, c], rs_send.at[d], rs_recv.at[d], {"gx": target}
        )

    def send_sq(d, carry):
        sq_copy(d).start()
        return carry

    lax.fori_loop(1, n, send_sq, 0)

    def project(c, carry):
        pltpu.make_async_copy(weights.at[c], weights.at[c], w_sem.at[c]).wait()
        result = jnp.dot(scaled[...], weights[c], preferred_element_type=jnp.float32)
        for g in range(n):
            part[g, c] = result[4 * g : 4 * g + 4]

        def send(d, inner):
            rs_copy(d, c).start()
            return inner

        lax.fori_loop(1, n, send, 0)
        return carry

    lax.fori_loop(0, chunks, project, 0)

    row_id = lax.broadcasted_iota(jnp.int32, (4, HEAD_SIZE), 0)
    first = positions_ref[2 * me]
    second = positions_ref[2 * me + 1]
    offsets = jnp.where(row_id < 2, first, second) + lax.rem(row_id, 2)
    angles = offsets.astype(jnp.float32) * freq_ref[...]
    lane = lax.broadcasted_iota(jnp.int32, (4, HEAD_SIZE), 1)
    cosine = jnp.cos(angles)
    sine = jnp.sin(angles)
    sine = jnp.where(lane < HEAD_SIZE // 2, -sine, sine)

    sq_recv[me] = sq_part[me]
    recv[me] = part[me]

    def arrive(d, carry):
        source = lax.rem(me + n - d, n)
        sq_copy(d).wait()
        whole = remote(
            part.at[lax.rem(me + d, n)],
            recv.at[source],
            rs_send.at[d],
            rs_recv.at[d],
            {"gx": lax.rem(me + d, n)},
        )
        whole.wait()
        return carry

    lax.fori_loop(1, n, arrive, 0)

    inverse = lax.rsqrt(jnp.sum(sq_recv[...], axis=0) / MODEL_WIDTH + 1e-05)
    heads_in_chunk = CHUNK // HEAD_SIZE
    for c in range(chunks):
        sums = jnp.sum(recv[:, c], axis=0)
        for k in range(heads_in_chunk):
            value = sums[:, k * HEAD_SIZE : (k + 1) * HEAD_SIZE] * inverse
            is_value = c == q_chunks and k >= heads_in_chunk // 2
            if not is_value:
                value = value * cosine + pltpu.roll(value, HEAD_SIZE // 2, 1) * sine
            if c < q_chunks:
                head = c * heads_in_chunk + k
                group, at = head // GROUP, 2 * (head % GROUP)
            else:
                group, at = k % 2, 48 if is_value else 32
            for r in range(2):
                turned[r, group, at : at + 2, :] = value[2 * r : 2 * r + 2]

    q_send[...] = turned[other].astype(jnp.bfloat16)
    swap = remote(q_send, q_all.at[core], q_ssem, q_rsem, {"yz": other})
    swap.start()
    q_all[core] = turned[core].astype(jnp.bfloat16)

    pltpu.make_async_copy(kc_hbm, kc, c_sem.at[0]).wait()
    pltpu.make_async_copy(vc_hbm, vc, c_sem.at[1]).wait()

    length = lengths_ref[0]
    scale = HEAD_SIZE ** (-0.5)
    queries = STEPS * GROUP
    slots = kc.shape[0]
    valid = lax.broadcasted_iota(jnp.int32, (queries, slots), 1) < length
    seen = lax.broadcasted_iota(jnp.int32, (queries, 16), 1) <= lax.rem(
        lax.broadcasted_iota(jnp.int32, (queries, 16), 0), 2
    )

    def attend(half):
        for i in range(2):
            block = q_all[half, i]
            q, kn, vn = block[:queries], block[32:48], block[48:64]
            at = pl.ds(pl.multiple_of((half * 2 + i) * HEAD_SIZE, HEAD_SIZE), HEAD_SIZE)
            cached = scale * lax.dot_general(
                q, kc[:, at], (((1,), (1,)), ((), ())), preferred_element_type=jnp.float32
            )
            recent = scale * lax.dot_general(
                q, kn, (((1,), (1,)), ((), ())), preferred_element_type=jnp.float32
            )
            cached = jnp.where(valid, cached, -jnp.inf)
            recent = jnp.where(seen, recent, -jnp.inf)
            highest = jnp.maximum(
                jnp.max(cached, axis=1, keepdims=True), jnp.max(recent, axis=1, keepdims=True)
            )
            cached = jnp.exp(cached - highest)
            recent = jnp.exp(recent - highest)
            total = jnp.sum(cached, axis=1, keepdims=True) + jnp.sum(
                recent, axis=1, keepdims=True
            )
            weighted = jnp.dot(
                cached.astype(jnp.bfloat16), vc[:, at], preferred_element_type=jnp.float32
            ) + jnp.dot(recent.astype(jnp.bfloat16), vn, preferred_element_type=jnp.float32)
            att[half, i * queries : (i + 1) * queries, :] = (weighted / total).astype(
                jnp.bfloat16
            )

    def spread_copy(t):
        target = lax.rem(flat + t, every)
        half = lax.rem(target, 2)
        return remote(
            att.at[half],
            gathered.at[flat],
            g_ssem.at[t],
            g_rsem.at[t],
            {"gx": target // 2, "yz": half},
        )

    attend(core)
    gathered[flat] = att[core]

    def spread_own(k, carry):
        spread_copy(2 * k).start()
        return carry

    lax.fori_loop(1, n, spread_own, 0)
    swap.wait()
    attend(other)

    def spread_other(k, carry):
        spread_copy(2 * k + 1).start()
        return carry

    lax.fori_loop(0, n, spread_other, 0)

    for half in range(2):
        for i in range(2):
            at = (half * 2 + i) * HEAD_SIZE
            block = q_all[half, i].astype(jnp.float32)
            newk_ref[:, at : at + HEAD_SIZE] = block[32:34].astype(jnp.bfloat16)
            newv_ref[:, at : at + HEAD_SIZE] = block[48:50].astype(jnp.bfloat16)

    def landed(t, carry):
        source = lax.rem(flat + every - t, every)
        target = lax.rem(flat + t, every)
        half = lax.rem(target, 2)
        remote(
            att.at[half],
            gathered.at[source],
            g_ssem.at[t],
            g_rsem.at[t],
            {"gx": target // 2, "yz": half},
        ).wait()
        return carry

    lax.fori_loop(1, every, landed, 0)

    block_rows = gathered.shape[1]
    for f in range(every):
        wide[f * block_rows : (f + 1) * block_rows, :] = gathered[f].astype(jnp.float32)
    for head in range(block_rows // STEPS):
        for s in range(STEPS):
            taken = wide[pl.ds(head * STEPS + s, every, stride=block_rows), :]
            lhs[s * every : (s + 1) * every, head * HEAD_SIZE : (head + 1) * HEAD_SIZE] = (
                taken.astype(jnp.bfloat16)
            )

    def final_copy(c):
        return remote(p_send.at[c], p_recv.at[c], p_ssem.at[c], p_rsem.at[c], {"yz": other})

    for c in range(OUT_PARTS):
        pltpu.make_async_copy(
            ow_hbm.at[:, c * out_cols : (c + 1) * out_cols], ow.at[c], o_sem.at[c]
        ).wait()
        p_send[c] = jnp.dot(lhs[...], ow[c], preferred_element_type=jnp.float32).astype(
            jnp.bfloat16
        )
        final_copy(c).start()
    for c in range(OUT_PARTS):
        final_copy(c).wait()
        both = p_send[c].astype(jnp.float32) + p_recv[c].astype(jnp.float32)
        at = slice(c * out_cols, (c + 1) * out_cols)
        for s in range(STEPS):
            mixed = x_ref[s, :, at].astype(jnp.float32) + both[s * every : (s + 1) * every]
            out_ref[s, :, at] = mixed.astype(jnp.bfloat16)


def per_device(
    hidden,
    norm_gain,
    query_weight,
    key_matrix,
    value_matrix,
    output_weight,
    key_cache_rows,
    value_cache_rows,
    lengths,
    positions,
):
    rows, width = hidden.shape[1], hidden.shape[2]
    n = lax.axis_size("gx")
    chunks = query_weight.shape[1] // CHUNK + 1
    slots, cache_cols = key_cache_rows.shape[1:]
    heads = query_weight.shape[1] // HEAD_SIZE
    half = HEAD_SIZE // 2
    freq = 500000.0 ** (-2.0 * jnp.arange(half, dtype=jnp.float32) / HEAD_SIZE)
    freq = jnp.concatenate([freq, freq])[None, :]
    ordered = hidden.transpose(1, 0, 2).reshape(rows * STEPS, width)
    out_cols = width // OUT_PARTS
    vmem = pl.BlockSpec(memory_space=pltpu.VMEM)
    smem = pl.BlockSpec(memory_space=pltpu.SMEM)
    hbm = pl.BlockSpec(memory_space=pl.ANY)
    bf16, f32 = jnp.bfloat16, jnp.float32
    dma = pltpu.SemaphoreType.DMA
    out, new_k, new_v = pl.pallas_call(
        functools.partial(kernel, n),
        out_shape=(
            jax.ShapeDtypeStruct((STEPS, rows, width), bf16),
            jax.ShapeDtypeStruct((STEPS, cache_cols), bf16),
            jax.ShapeDtypeStruct((STEPS, cache_cols), bf16),
        ),
        in_specs=[vmem, vmem, vmem, vmem, smem, smem] + [hbm] * 6,
        out_specs=(vmem, vmem, vmem),
        scratch_shapes=[
            pltpu.VMEM((chunks, width, CHUNK), bf16),
            pltpu.VMEM((slots, cache_cols), bf16),
            pltpu.VMEM((slots, cache_cols), bf16),
            pltpu.VMEM((OUT_PARTS, output_weight.shape[0], out_cols), bf16),
            pltpu.VMEM((rows * STEPS, width), bf16),
            pltpu.VMEM((n, chunks, 4, CHUNK), f32),
            pltpu.VMEM((n, chunks, 4, CHUNK), f32),
            pltpu.VMEM((n, 4, HEAD_SIZE), f32),
            pltpu.VMEM((n, 4, HEAD_SIZE), f32),
            pltpu.VMEM((2, 2, 64, HEAD_SIZE), f32),
            pltpu.VMEM((2, 64, HEAD_SIZE), bf16),
            pltpu.VMEM((2, 2, 64, HEAD_SIZE), bf16),
            pltpu.VMEM((2, heads * STEPS, HEAD_SIZE), bf16),
            pltpu.VMEM((2 * n, heads * STEPS, HEAD_SIZE), bf16),
            pltpu.VMEM((2 * n * heads * STEPS, HEAD_SIZE), f32),
            pltpu.VMEM((rows * STEPS, heads * HEAD_SIZE), bf16),
            pltpu.VMEM((OUT_PARTS, rows * STEPS, out_cols), bf16),
            pltpu.VMEM((OUT_PARTS, rows * STEPS, out_cols), bf16),
            dma((chunks,)),
            dma((2,)),
            dma((OUT_PARTS,)),
            dma((n,)),
            dma((n,)),
            dma((n,)),
            dma((n,)),
            dma,
            dma,
            dma((2 * n,)),
            dma((2 * n,)),
            dma((OUT_PARTS,)),
            dma((OUT_PARTS,)),
        ],
        compiler_params=pltpu.CompilerParams(
            collective_id=0, has_side_effects=True, vmem_limit_bytes=56 * 2**20
        ),
    )(
        ordered,
        hidden,
        norm_gain[None, :],
        freq,
        lengths,
        positions,
        query_weight,
        key_matrix,
        value_matrix,
        output_weight,
        key_cache_rows.reshape(slots, cache_cols),
        value_cache_rows.reshape(slots, cache_cols),
    )
    return (out, new_k[:, None, :], new_v[:, None, :])


def solution(mesh):
    in_specs = (
        P(None, "rep", "gx"),
        P("gx"),
        P("gx", "yz"),
        P("gx", "yz"),
        P("gx", "yz"),
        P("yz", "gx"),
        P(("rep", "gx", "yz"), None, None),
        P(("rep", "gx", "yz"), None, None),
        P(("rep", "gx", "yz")),
        P("rep"),
    )
    out_specs = (
        P(None, "rep", "gx"),
        P(None, ("rep", "gx", "yz"), None),
        P(None, ("rep", "gx", "yz"), None),
    )
    return jax.shard_map(
        per_device, mesh=mesh, in_specs=in_specs, out_specs=out_specs, check_vma=False
    )
```

```python
import functools
import math

import jax
import jax.numpy as jnp
from jax import lax
from jax.experimental import pallas as pl
from jax.experimental.pallas import tpu as pltpu
from jax.sharding import PartitionSpec as P

MODEL_WIDTH = 16384
HEAD_SIZE = 128
STEPS = 2
GROUP = 16
CHUNK = 512
OUT_PARTS = 4
LAG = 2
MESH = pl.DeviceIdType.MESH


def remote(src, dst, send_sem, recv_sem, device):
    return pltpu.make_async_remote_copy(
        src_ref=src,
        dst_ref=dst,
        send_sem=send_sem,
        recv_sem=recv_sem,
        device_id=device,
        device_id_type=MESH,
    )


def kernel(
    n,
    x_ref,
    gain_ref,
    lengths_ref,
    positions_ref,
    qw_hbm,
    kw_hbm,
    vw_hbm,
    ow_hbm,
    kc_hbm,
    vc_hbm,
    out_ref,
    newk_ref,
    newv_ref,
    weights,
    kc,
    vc,
    ow,
    scaled,
    part,
    mate_part,
    mid,
    recv,
    sq_part,
    sq_recv,
    turned,
    q_send,
    q_all,
    att,
    gathered,
    wide,
    lhs,
    p_send,
    p_recv,
    w_sem,
    c_sem,
    o_sem,
    mate_send,
    mate_recv,
    rs_send,
    rs_recv,
    sq_ssem,
    sq_rsem,
    q_ssem,
    q_rsem,
    g_ssem,
    g_rsem,
    p_ssem,
    p_rsem,
):
    me = lax.axis_index("gx")
    core = lax.axis_index("yz")
    other = 1 - core
    flat = me * 2 + core
    chunks = weights.shape[0]
    q_chunks = chunks - 1
    key_cols = kw_hbm.shape[1]
    out_cols = ow.shape[2]
    every = 2 * n
    pairs = n // 2
    high, low = me // 2, lax.rem(me, 2)
    mate = me + 1 - 2 * low

    for c in range(q_chunks):
        pltpu.make_async_copy(
            qw_hbm.at[:, c * CHUNK : (c + 1) * CHUNK], weights.at[c], w_sem.at[c]
        ).start()
    last = weights.at[q_chunks]
    pltpu.make_async_copy(kw_hbm, last.at[:, :key_cols], w_sem.at[q_chunks]).start()
    pltpu.make_async_copy(vw_hbm, last.at[:, key_cols:], w_sem.at[q_chunks]).start()
    pltpu.make_async_copy(kc_hbm, kc, c_sem.at[0]).start()
    pltpu.make_async_copy(vc_hbm, vc, c_sem.at[1]).start()
    for c in range(OUT_PARTS):
        pltpu.make_async_copy(
            ow_hbm.at[:, c * out_cols : (c + 1) * out_cols], ow.at[c], o_sem.at[c]
        ).start()

    barrier = pltpu.get_barrier_semaphore()

    def greet(t, carry):
        target = lax.rem(flat + t, every)
        pl.semaphore_signal(
            barrier,
            inc=1,
            device_id={"gx": target // 2, "yz": lax.rem(target, 2)},
            device_id_type=MESH,
        )
        return carry

    lax.fori_loop(1, every, greet, 0)

    for step in range(STEPS):
        xf = x_ref[step].astype(jnp.float32)
        squares = jnp.sum(xf * xf, axis=1, keepdims=True)
        squares = jnp.broadcast_to(squares, (every, HEAD_SIZE))
        scaled[step * every : (step + 1) * every] = (xf * gain_ref[...]).astype(jnp.bfloat16)
        for g in range(n):
            sq_part[g, 2 * step : 2 * step + 2] = squares[2 * g : 2 * g + 2]
    turned[...] = jnp.zeros_like(turned)

    pl.semaphore_wait(barrier, every - 1)

    def sq_copy(d):
        target = lax.rem(me + d, n)
        return remote(
            sq_part.at[target], sq_recv.at[me], sq_ssem.at[d], sq_rsem.at[d], {"gx": target}
        )

    def mate_copy(c):
        return remote(
            part.at[1 - low, c], mate_part.at[c], mate_send.at[c], mate_recv.at[c], {"gx": mate}
        )

    def rs_copy(d, c):
        target = lax.rem(high + d, pairs)
        return remote(
            mid.at[target, c],
            recv.at[high, c],
            rs_send.at[d],
            rs_recv.at[d],
            {"gx": target * 2 + low},
        )

    def send_sq(d, carry):
        sq_copy(d).start()
        return carry

    lax.fori_loop(1, n, send_sq, 0)

    def project(c):
        pltpu.make_async_copy(weights.at[c], weights.at[c], w_sem.at[c]).wait()
        result = jnp.dot(scaled[...], weights[c], preferred_element_type=jnp.float32)
        for g in range(n):
            for step in range(STEPS):
                at = step * every + 2 * g
                part[g % 2, c, g // 2, 2 * step : 2 * step + 2] = result[at : at + 2]
        mate_copy(c).start()

    def add_mate(c):
        mate_copy(c).wait()
        for p in range(pairs):
            mid[p, c] = part[low, c, p] + mate_part[c, p]

        def send(d, inner):
            rs_copy(d, c).start()
            return inner

        lax.fori_loop(1, pairs, send, 0)

    def stage(c, carry):
        pl.when(c < chunks)(lambda: project(c))
        pl.when(c >= LAG)(lambda: add_mate(c - LAG))
        return carry

    lax.fori_loop(0, chunks + LAG, stage, 0)

    row_id = lax.broadcasted_iota(jnp.int32, (4, HEAD_SIZE), 0)
    first = positions_ref[2 * me]
    second = positions_ref[2 * me + 1]
    offsets = jnp.where(lax.rem(row_id, 2) == 0, first, second) + row_id // 2
    lane = lax.broadcasted_iota(jnp.int32, (4, HEAD_SIZE), 1)
    index = lax.rem(lane, HEAD_SIZE // 2).astype(jnp.float32)
    freq = jnp.exp(index * (-2.0 * math.log(500000.0) / HEAD_SIZE))
    angles = offsets.astype(jnp.float32) * freq
    cosine = jnp.cos(angles)
    sine = jnp.sin(angles)
    sine = jnp.where(lane < HEAD_SIZE // 2, -sine, sine)

    sq_recv[me] = sq_part[me]
    recv[high] = mid[high]

    def arrive_sq(d, carry):
        sq_copy(d).wait()
        return carry

    lax.fori_loop(1, n, arrive_sq, 0)

    def arrive(d, carry):
        target = lax.rem(high + d, pairs)
        remote(
            mid.at[target],
            recv.at[lax.rem(high + pairs - d, pairs)],
            rs_send.at[d],
            rs_recv.at[d],
            {"gx": target * 2 + low},
        ).wait()
        return carry

    lax.fori_loop(1, pairs, arrive, 0)

    inverse = lax.rsqrt(jnp.sum(sq_recv[...], axis=0) / MODEL_WIDTH + 1e-05)
    heads_in_chunk = CHUNK // HEAD_SIZE
    for c in range(chunks):
        sums = jnp.sum(recv[:, c], axis=0)
        for k in range(heads_in_chunk):
            value = sums[:, k * HEAD_SIZE : (k + 1) * HEAD_SIZE] * inverse
            is_value = c == q_chunks and k >= heads_in_chunk // 2
            if not is_value:
                value = value * cosine + pltpu.roll(value, HEAD_SIZE // 2, 1) * sine
            if c < q_chunks:
                head = c * heads_in_chunk + k
                group, at = head // GROUP, 2 * (head % GROUP)
            else:
                group, at = k % 2, 48 if is_value else 32
            for r in range(2):
                for step in range(STEPS):
                    turned[r, group, at + step : at + step + 1, :] = value[
                        2 * step + r : 2 * step + r + 1
                    ]

    q_send[...] = turned[other].astype(jnp.bfloat16)
    swap = remote(q_send, q_all.at[core], q_ssem, q_rsem, {"yz": other})
    swap.start()
    q_all[core] = turned[core].astype(jnp.bfloat16)

    pltpu.make_async_copy(kc_hbm, kc, c_sem.at[0]).wait()
    pltpu.make_async_copy(vc_hbm, vc, c_sem.at[1]).wait()

    length = lengths_ref[0]
    scale = HEAD_SIZE ** (-0.5)
    queries = STEPS * GROUP
    slots = kc.shape[0]
    valid = lax.broadcasted_iota(jnp.int32, (queries, slots), 1) < length
    seen = lax.broadcasted_iota(jnp.int32, (queries, 16), 1) <= lax.rem(
        lax.broadcasted_iota(jnp.int32, (queries, 16), 0), 2
    )

    def attend(half):
        for i in range(2):
            block = q_all[half, i]
            q, kn, vn = block[:queries], block[32:48], block[48:64]
            at = pl.ds(pl.multiple_of((half * 2 + i) * HEAD_SIZE, HEAD_SIZE), HEAD_SIZE)
            cached = scale * lax.dot_general(
                q, kc[:, at], (((1,), (1,)), ((), ())), preferred_element_type=jnp.float32
            )
            recent = scale * lax.dot_general(
                q, kn, (((1,), (1,)), ((), ())), preferred_element_type=jnp.float32
            )
            cached = jnp.where(valid, cached, -jnp.inf)
            recent = jnp.where(seen, recent, -jnp.inf)
            highest = jnp.maximum(
                jnp.max(cached, axis=1, keepdims=True), jnp.max(recent, axis=1, keepdims=True)
            )
            cached = jnp.exp(cached - highest)
            recent = jnp.exp(recent - highest)
            total = jnp.sum(cached, axis=1, keepdims=True) + jnp.sum(
                recent, axis=1, keepdims=True
            )
            weighted = jnp.dot(
                cached.astype(jnp.bfloat16), vc[:, at], preferred_element_type=jnp.float32
            ) + jnp.dot(recent.astype(jnp.bfloat16), vn, preferred_element_type=jnp.float32)
            att[half, i * queries : (i + 1) * queries, :] = (weighted / total).astype(
                jnp.bfloat16
            )

    def spread_copy(t):
        target = lax.rem(flat + t, every)
        half = lax.rem(target, 2)
        return remote(
            att.at[half],
            gathered.at[flat],
            g_ssem.at[t],
            g_rsem.at[t],
            {"gx": target // 2, "yz": half},
        )

    attend(core)
    gathered[flat] = att[core]

    def spread_own(k, carry):
        spread_copy(2 * k).start()
        return carry

    lax.fori_loop(1, n, spread_own, 0)
    swap.wait()
    attend(other)

    def spread_other(k, carry):
        spread_copy(2 * k + 1).start()
        return carry

    lax.fori_loop(0, n, spread_other, 0)

    for half in range(2):
        for i in range(2):
            at = (half * 2 + i) * HEAD_SIZE
            block = q_all[half, i].astype(jnp.float32)
            newk_ref[:, at : at + HEAD_SIZE] = block[32:34].astype(jnp.bfloat16)
            newv_ref[:, at : at + HEAD_SIZE] = block[48:50].astype(jnp.bfloat16)

    def landed(t, carry):
        source = lax.rem(flat + every - t, every)
        target = lax.rem(flat + t, every)
        half = lax.rem(target, 2)
        remote(
            att.at[half],
            gathered.at[source],
            g_ssem.at[t],
            g_rsem.at[t],
            {"gx": target // 2, "yz": half},
        ).wait()
        return carry

    lax.fori_loop(1, every, landed, 0)

    block_rows = gathered.shape[1]
    for f in range(every):
        wide[f * block_rows : (f + 1) * block_rows, :] = gathered[f].astype(jnp.float32)
    for head in range(block_rows // STEPS):
        for s in range(STEPS):
            taken = wide[pl.ds(head * STEPS + s, every, stride=block_rows), :]
            lhs[s * every : (s + 1) * every, head * HEAD_SIZE : (head + 1) * HEAD_SIZE] = (
                taken.astype(jnp.bfloat16)
            )

    def final_copy(c):
        return remote(p_send.at[c], p_recv.at[c], p_ssem.at[c], p_rsem.at[c], {"yz": other})

    for c in range(OUT_PARTS):
        pltpu.make_async_copy(
            ow_hbm.at[:, c * out_cols : (c + 1) * out_cols], ow.at[c], o_sem.at[c]
        ).wait()
        p_send[c] = jnp.dot(lhs[...], ow[c], preferred_element_type=jnp.float32).astype(
            jnp.bfloat16
        )
        final_copy(c).start()
    for c in range(OUT_PARTS):
        final_copy(c).wait()
        both = p_send[c].astype(jnp.float32) + p_recv[c].astype(jnp.float32)
        at = slice(c * out_cols, (c + 1) * out_cols)
        for s in range(STEPS):
            mixed = x_ref[s, :, at].astype(jnp.float32) + both[s * every : (s + 1) * every]
            out_ref[s, :, at] = mixed.astype(jnp.bfloat16)


def hand_over(out_in, k_in, v_in, out, k, v):
    out[...] = out_in[...]
    k[...] = k_in[...]
    v[...] = v_in[...]


def per_device(
    hidden,
    norm_gain,
    query_weight,
    key_matrix,
    value_matrix,
    output_weight,
    key_cache_rows,
    value_cache_rows,
    lengths,
    positions,
):
    rows, width = hidden.shape[1], hidden.shape[2]
    n = lax.axis_size("gx")
    chunks = query_weight.shape[1] // CHUNK + 1
    slots, cache_cols = key_cache_rows.shape[1:]
    heads = query_weight.shape[1] // HEAD_SIZE
    out_cols = width // OUT_PARTS
    vmem = pl.BlockSpec(memory_space=pltpu.VMEM)
    smem = pl.BlockSpec(memory_space=pltpu.SMEM)
    hbm = pl.BlockSpec(memory_space=pl.ANY)
    bf16, f32 = jnp.bfloat16, jnp.float32
    dma = pltpu.SemaphoreType.DMA
    out, new_k, new_v = pl.pallas_call(
        functools.partial(kernel, n),
        out_shape=(
            jax.ShapeDtypeStruct((STEPS, rows, width), bf16),
            jax.ShapeDtypeStruct((STEPS, cache_cols), bf16),
            jax.ShapeDtypeStruct((STEPS, cache_cols), bf16),
        ),
        in_specs=[vmem, vmem, smem, smem] + [hbm] * 6,
        out_specs=(vmem, vmem, vmem),
        scratch_shapes=[
            pltpu.VMEM((chunks, width, CHUNK), bf16),
            pltpu.VMEM((slots, cache_cols), bf16),
            pltpu.VMEM((slots, cache_cols), bf16),
            pltpu.VMEM((OUT_PARTS, output_weight.shape[0], out_cols), bf16),
            pltpu.VMEM((rows * STEPS, width), bf16),
            pltpu.VMEM((2, chunks, n // 2, 4, CHUNK), f32),
            pltpu.VMEM((chunks, n // 2, 4, CHUNK), f32),
            pltpu.VMEM((n // 2, chunks, 4, CHUNK), f32),
            pltpu.VMEM((n // 2, chunks, 4, CHUNK), f32),
            pltpu.VMEM((n, 4, HEAD_SIZE), f32),
            pltpu.VMEM((n, 4, HEAD_SIZE), f32),
            pltpu.VMEM((2, 2, 64, HEAD_SIZE), f32),
            pltpu.VMEM((2, 64, HEAD_SIZE), bf16),
            pltpu.VMEM((2, 2, 64, HEAD_SIZE), bf16),
            pltpu.VMEM((2, heads * STEPS, HEAD_SIZE), bf16),
            pltpu.VMEM((2 * n, heads * STEPS, HEAD_SIZE), bf16),
            pltpu.VMEM((2 * n * heads * STEPS, HEAD_SIZE), f32),
            pltpu.VMEM((rows * STEPS, heads * HEAD_SIZE), bf16),
            pltpu.VMEM((OUT_PARTS, rows * STEPS, out_cols), bf16),
            pltpu.VMEM((OUT_PARTS, rows * STEPS, out_cols), bf16),
            dma((chunks,)),
            dma((2,)),
            dma((OUT_PARTS,)),
            dma((chunks,)),
            dma((chunks,)),
            dma((n // 2,)),
            dma((n // 2,)),
            dma((n,)),
            dma((n,)),
            dma,
            dma,
            dma((2 * n,)),
            dma((2 * n,)),
            dma((OUT_PARTS,)),
            dma((OUT_PARTS,)),
        ],
        compiler_params=pltpu.CompilerParams(
            collective_id=0, has_side_effects=True, vmem_limit_bytes=56 * 2**20
        ),
    )(
        hidden,
        norm_gain[None, :],
        lengths,
        positions,
        query_weight,
        key_matrix,
        value_matrix,
        output_weight,
        key_cache_rows.reshape(slots, cache_cols),
        value_cache_rows.reshape(slots, cache_cols),
    )
    out, new_k, new_v = pl.pallas_call(
        hand_over,
        out_shape=(
            jax.ShapeDtypeStruct(out.shape, bf16),
            jax.ShapeDtypeStruct(new_k.shape, bf16),
            jax.ShapeDtypeStruct(new_v.shape, bf16),
        ),
        in_specs=[vmem] * 3,
        out_specs=(vmem,) * 3,
    )(out, new_k, new_v)
    return (out, new_k[:, None, :], new_v[:, None, :])


def solution(mesh):
    in_specs = (
        P(None, "rep", "gx"),
        P("gx"),
        P("gx", "yz"),
        P("gx", "yz"),
        P("gx", "yz"),
        P("yz", "gx"),
        P(("rep", "gx", "yz"), None, None),
        P(("rep", "gx", "yz"), None, None),
        P(("rep", "gx", "yz")),
        P("rep"),
    )
    out_specs = (
        P(None, "rep", "gx"),
        P(None, ("rep", "gx", "yz"), None),
        P(None, ("rep", "gx", "yz"), None),
    )
    return jax.shard_map(
        per_device, mesh=mesh, in_specs=in_specs, out_specs=out_specs, check_vma=False
    )
```

```python
import functools
import math

import jax
import jax.numpy as jnp
from jax import lax
from jax.experimental import pallas as pl
from jax.experimental.pallas import tpu as pltpu
from jax.sharding import PartitionSpec as P

MODEL_WIDTH = 16384
HEAD_SIZE = 128
STEPS = 2
GROUP = 16
CHUNK = 512
OUT_PARTS = 4
LAG = 2
AHEAD = 4
MESH = pl.DeviceIdType.MESH


def remote(src, dst, send_sem, recv_sem, device):
    return pltpu.make_async_remote_copy(
        src_ref=src,
        dst_ref=dst,
        send_sem=send_sem,
        recv_sem=recv_sem,
        device_id=device,
        device_id_type=MESH,
    )


def kernel(
    n,
    x_ref,
    gain_ref,
    lengths_ref,
    positions_ref,
    qw_hbm,
    kw_hbm,
    vw_hbm,
    ow_hbm,
    kc_hbm,
    vc_hbm,
    out_ref,
    newk_ref,
    newv_ref,
    weights,
    kc,
    vc,
    ow,
    scaled,
    part,
    mate_part,
    mid,
    recv,
    sq_part,
    sq_recv,
    turned,
    q_send,
    q_all,
    att,
    gathered,
    wide,
    lhs,
    p_send,
    p_recv,
    w_sem,
    c_sem,
    o_sem,
    mate_send,
    mate_recv,
    rs_send,
    rs_recv,
    sq_ssem,
    sq_rsem,
    q_ssem,
    q_rsem,
    g_ssem,
    g_rsem,
    p_ssem,
    p_rsem,
):
    me = lax.axis_index("gx")
    core = lax.axis_index("yz")
    other = 1 - core
    flat = me * 2 + core
    chunks = weights.shape[0]
    q_chunks = chunks - 1
    key_cols = kw_hbm.shape[1]
    out_cols = ow.shape[2]
    every = 2 * n
    pairs = n // 2
    high, low = me // 2, lax.rem(me, 2)
    mate = me + 1 - 2 * low

    def fetch_query(c):
        at = pl.ds(pl.multiple_of(c * CHUNK, CHUNK), CHUNK)
        pltpu.make_async_copy(qw_hbm.at[:, at], weights.at[c], w_sem.at[c]).start()

    def fetch_new():
        last = weights.at[q_chunks]
        pltpu.make_async_copy(kw_hbm, last.at[:, :key_cols], w_sem.at[q_chunks]).start()
        pltpu.make_async_copy(vw_hbm, last.at[:, key_cols:], w_sem.at[q_chunks]).start()

    def fetch_caches():
        pltpu.make_async_copy(kc_hbm, kc, c_sem.at[0]).start()
        pltpu.make_async_copy(vc_hbm, vc, c_sem.at[1]).start()

    def fetch_output(c):
        pltpu.make_async_copy(
            ow_hbm.at[:, c * out_cols : (c + 1) * out_cols], ow.at[c], o_sem.at[c]
        ).start()

    def fetch_later(c):
        pl.when(c + AHEAD < q_chunks)(lambda: fetch_query(c + AHEAD))
        pl.when(c + AHEAD == q_chunks)(fetch_new)
        pl.when(c + AHEAD == q_chunks + 1)(fetch_caches)
        for k in range(OUT_PARTS):
            turn = min(q_chunks + 2 + k - AHEAD, chunks - 1)
            pl.when(c == turn)(functools.partial(fetch_output, k))

    for c in range(AHEAD):
        fetch_query(c)

    barrier = pltpu.get_barrier_semaphore()

    def greet(t, carry):
        target = lax.rem(flat + t, every)
        pl.semaphore_signal(
            barrier,
            inc=1,
            device_id={"gx": target // 2, "yz": lax.rem(target, 2)},
            device_id_type=MESH,
        )
        return carry

    lax.fori_loop(1, every, greet, 0)

    for step in range(STEPS):
        xf = x_ref[step].astype(jnp.float32)
        squares = jnp.sum(xf * xf, axis=1, keepdims=True)
        squares = jnp.broadcast_to(squares, (every, HEAD_SIZE))
        scaled[step * every : (step + 1) * every] = (xf * gain_ref[...]).astype(jnp.bfloat16)
        for g in range(n):
            sq_part[g, 2 * step : 2 * step + 2] = squares[2 * g : 2 * g + 2]
    turned[...] = jnp.zeros_like(turned)

    pl.semaphore_wait(barrier, every - 1)

    def sq_copy(d):
        target = lax.rem(me + d, n)
        return remote(
            sq_part.at[target], sq_recv.at[me], sq_ssem.at[d], sq_rsem.at[d], {"gx": target}
        )

    def mate_copy(c):
        return remote(
            part.at[1 - low, c], mate_part.at[c], mate_send.at[c], mate_recv.at[c], {"gx": mate}
        )

    def rs_copy(d, c):
        target = lax.rem(high + d, pairs)
        return remote(
            mid.at[target, c],
            recv.at[high, c],
            rs_send.at[d],
            rs_recv.at[d],
            {"gx": target * 2 + low},
        )

    def send_sq(d, carry):
        sq_copy(d).start()
        return carry

    lax.fori_loop(1, n, send_sq, 0)

    def project(c):
        pltpu.make_async_copy(weights.at[c], weights.at[c], w_sem.at[c]).wait()
        fetch_later(c)
        result = jnp.dot(scaled[...], weights[c], preferred_element_type=jnp.float32)
        for g in range(n):
            for step in range(STEPS):
                at = step * every + 2 * g
                part[g % 2, c, g // 2, 2 * step : 2 * step + 2] = result[at : at + 2]
        mate_copy(c).start()

    def add_mate(c):
        mate_copy(c).wait()
        for p in range(pairs):
            mid[p, c] = part[low, c, p] + mate_part[c, p]

        def send(d, inner):
            rs_copy(d, c).start()
            return inner

        lax.fori_loop(1, pairs, send, 0)

    def stage(c, carry):
        pl.when(c < chunks)(lambda: project(c))
        pl.when(c >= LAG)(lambda: add_mate(c - LAG))
        return carry

    lax.fori_loop(0, chunks + LAG, stage, 0)

    row_id = lax.broadcasted_iota(jnp.int32, (4, HEAD_SIZE), 0)
    first = positions_ref[2 * me]
    second = positions_ref[2 * me + 1]
    offsets = jnp.where(lax.rem(row_id, 2) == 0, first, second) + row_id // 2
    lane = lax.broadcasted_iota(jnp.int32, (4, HEAD_SIZE), 1)
    index = lax.rem(lane, HEAD_SIZE // 2).astype(jnp.float32)
    freq = jnp.exp(index * (-2.0 * math.log(500000.0) / HEAD_SIZE))
    angles = offsets.astype(jnp.float32) * freq
    cosine = jnp.cos(angles)
    sine = jnp.sin(angles)
    sine = jnp.where(lane < HEAD_SIZE // 2, -sine, sine)

    sq_recv[me] = sq_part[me]
    recv[high] = mid[high]

    def arrive_sq(d, carry):
        sq_copy(d).wait()
        return carry

    lax.fori_loop(1, n, arrive_sq, 0)

    def arrive(d, carry):
        target = lax.rem(high + d, pairs)
        remote(
            mid.at[target],
            recv.at[lax.rem(high + pairs - d, pairs)],
            rs_send.at[d],
            rs_recv.at[d],
            {"gx": target * 2 + low},
        ).wait()
        return carry

    lax.fori_loop(1, pairs, arrive, 0)

    inverse = lax.rsqrt(jnp.sum(sq_recv[...], axis=0) / MODEL_WIDTH + 1e-05)
    heads_in_chunk = CHUNK // HEAD_SIZE
    for c in range(chunks):
        sums = jnp.sum(recv[:, c], axis=0)
        for k in range(heads_in_chunk):
            value = sums[:, k * HEAD_SIZE : (k + 1) * HEAD_SIZE] * inverse
            is_value = c == q_chunks and k >= heads_in_chunk // 2
            if not is_value:
                value = value * cosine + pltpu.roll(value, HEAD_SIZE // 2, 1) * sine
            if c < q_chunks:
                head = c * heads_in_chunk + k
                group, at = head // GROUP, 2 * (head % GROUP)
            else:
                group, at = k % 2, 48 if is_value else 32
            for r in range(2):
                for step in range(STEPS):
                    turned[r, group, at + step : at + step + 1, :] = value[
                        2 * step + r : 2 * step + r + 1
                    ]

    q_send[...] = turned[other].astype(jnp.bfloat16)
    swap = remote(q_send, q_all.at[core], q_ssem, q_rsem, {"yz": other})
    swap.start()
    q_all[core] = turned[core].astype(jnp.bfloat16)

    pltpu.make_async_copy(kc_hbm, kc, c_sem.at[0]).wait()
    pltpu.make_async_copy(vc_hbm, vc, c_sem.at[1]).wait()

    length = lengths_ref[0]
    scale = HEAD_SIZE ** (-0.5)
    queries = STEPS * GROUP
    slots = kc.shape[0]
    valid = lax.broadcasted_iota(jnp.int32, (queries, slots), 1) < length
    seen = lax.broadcasted_iota(jnp.int32, (queries, 16), 1) <= lax.rem(
        lax.broadcasted_iota(jnp.int32, (queries, 16), 0), 2
    )

    def attend(half):
        for i in range(2):
            block = q_all[half, i]
            q, kn, vn = block[:queries], block[32:48], block[48:64]
            at = pl.ds(pl.multiple_of((half * 2 + i) * HEAD_SIZE, HEAD_SIZE), HEAD_SIZE)
            cached = scale * lax.dot_general(
                q, kc[:, at], (((1,), (1,)), ((), ())), preferred_element_type=jnp.float32
            )
            recent = scale * lax.dot_general(
                q, kn, (((1,), (1,)), ((), ())), preferred_element_type=jnp.float32
            )
            cached = jnp.where(valid, cached, -jnp.inf)
            recent = jnp.where(seen, recent, -jnp.inf)
            highest = jnp.maximum(
                jnp.max(cached, axis=1, keepdims=True), jnp.max(recent, axis=1, keepdims=True)
            )
            cached = jnp.exp(cached - highest)
            recent = jnp.exp(recent - highest)
            total = jnp.sum(cached, axis=1, keepdims=True) + jnp.sum(
                recent, axis=1, keepdims=True
            )
            weighted = jnp.dot(
                cached.astype(jnp.bfloat16), vc[:, at], preferred_element_type=jnp.float32
            ) + jnp.dot(recent.astype(jnp.bfloat16), vn, preferred_element_type=jnp.float32)
            att[half, i * queries : (i + 1) * queries, :] = (weighted / total).astype(
                jnp.bfloat16
            )

    def spread_copy(t):
        target = lax.rem(flat + t, every)
        half = lax.rem(target, 2)
        return remote(
            att.at[half],
            gathered.at[flat],
            g_ssem.at[t],
            g_rsem.at[t],
            {"gx": target // 2, "yz": half},
        )

    attend(core)
    gathered[flat] = att[core]

    def spread_own(k, carry):
        spread_copy(2 * k).start()
        return carry

    lax.fori_loop(1, n, spread_own, 0)
    swap.wait()
    attend(other)

    def spread_other(k, carry):
        spread_copy(2 * k + 1).start()
        return carry

    lax.fori_loop(0, n, spread_other, 0)

    for half in range(2):
        for i in range(2):
            at = (half * 2 + i) * HEAD_SIZE
            block = q_all[half, i].astype(jnp.float32)
            newk_ref[:, at : at + HEAD_SIZE] = block[32:34].astype(jnp.bfloat16)
            newv_ref[:, at : at + HEAD_SIZE] = block[48:50].astype(jnp.bfloat16)

    def landed(t, carry):
        source = lax.rem(flat + every - t, every)
        target = lax.rem(flat + t, every)
        half = lax.rem(target, 2)
        remote(
            att.at[half],
            gathered.at[source],
            g_ssem.at[t],
            g_rsem.at[t],
            {"gx": target // 2, "yz": half},
        ).wait()
        return carry

    lax.fori_loop(1, every, landed, 0)

    block_rows = gathered.shape[1]
    for f in range(every):
        wide[f * block_rows : (f + 1) * block_rows, :] = gathered[f].astype(jnp.float32)
    for head in range(block_rows // STEPS):
        for s in range(STEPS):
            taken = wide[pl.ds(head * STEPS + s, every, stride=block_rows), :]
            lhs[s * every : (s + 1) * every, head * HEAD_SIZE : (head + 1) * HEAD_SIZE] = (
                taken.astype(jnp.bfloat16)
            )

    def final_copy(c):
        return remote(p_send.at[c], p_recv.at[c], p_ssem.at[c], p_rsem.at[c], {"yz": other})

    for c in range(OUT_PARTS):
        pltpu.make_async_copy(
            ow_hbm.at[:, c * out_cols : (c + 1) * out_cols], ow.at[c], o_sem.at[c]
        ).wait()
        p_send[c] = jnp.dot(lhs[...], ow[c], preferred_element_type=jnp.float32).astype(
            jnp.bfloat16
        )
        final_copy(c).start()
    for c in range(OUT_PARTS):
        final_copy(c).wait()
        both = p_send[c].astype(jnp.float32) + p_recv[c].astype(jnp.float32)
        at = slice(c * out_cols, (c + 1) * out_cols)
        for s in range(STEPS):
            mixed = x_ref[s, :, at].astype(jnp.float32) + both[s * every : (s + 1) * every]
            out_ref[s, :, at] = mixed.astype(jnp.bfloat16)


def hand_over(out_in, k_in, v_in, out, k, v):
    out[...] = out_in[...]
    k[...] = k_in[...]
    v[...] = v_in[...]


def per_device(
    hidden,
    norm_gain,
    query_weight,
    key_matrix,
    value_matrix,
    output_weight,
    key_cache_rows,
    value_cache_rows,
    lengths,
    positions,
):
    rows, width = hidden.shape[1], hidden.shape[2]
    n = lax.axis_size("gx")
    chunks = query_weight.shape[1] // CHUNK + 1
    slots, cache_cols = key_cache_rows.shape[1:]
    heads = query_weight.shape[1] // HEAD_SIZE
    out_cols = width // OUT_PARTS
    vmem = pl.BlockSpec(memory_space=pltpu.VMEM)
    smem = pl.BlockSpec(memory_space=pltpu.SMEM)
    hbm = pl.BlockSpec(memory_space=pl.ANY)
    bf16, f32 = jnp.bfloat16, jnp.float32
    dma = pltpu.SemaphoreType.DMA
    out, new_k, new_v = pl.pallas_call(
        functools.partial(kernel, n),
        out_shape=(
            jax.ShapeDtypeStruct((STEPS, rows, width), bf16),
            jax.ShapeDtypeStruct((STEPS, cache_cols), bf16),
            jax.ShapeDtypeStruct((STEPS, cache_cols), bf16),
        ),
        in_specs=[vmem, vmem, smem, smem] + [hbm] * 6,
        out_specs=(vmem, vmem, vmem),
        scratch_shapes=[
            pltpu.VMEM((chunks, width, CHUNK), bf16),
            pltpu.VMEM((slots, cache_cols), bf16),
            pltpu.VMEM((slots, cache_cols), bf16),
            pltpu.VMEM((OUT_PARTS, output_weight.shape[0], out_cols), bf16),
            pltpu.VMEM((rows * STEPS, width), bf16),
            pltpu.VMEM((2, chunks, n // 2, 4, CHUNK), f32),
            pltpu.VMEM((chunks, n // 2, 4, CHUNK), f32),
            pltpu.VMEM((n // 2, chunks, 4, CHUNK), f32),
            pltpu.VMEM((n // 2, chunks, 4, CHUNK), f32),
            pltpu.VMEM((n, 4, HEAD_SIZE), f32),
            pltpu.VMEM((n, 4, HEAD_SIZE), f32),
            pltpu.VMEM((2, 2, 64, HEAD_SIZE), f32),
            pltpu.VMEM((2, 64, HEAD_SIZE), bf16),
            pltpu.VMEM((2, 2, 64, HEAD_SIZE), bf16),
            pltpu.VMEM((2, heads * STEPS, HEAD_SIZE), bf16),
            pltpu.VMEM((2 * n, heads * STEPS, HEAD_SIZE), bf16),
            pltpu.VMEM((2 * n * heads * STEPS, HEAD_SIZE), f32),
            pltpu.VMEM((rows * STEPS, heads * HEAD_SIZE), bf16),
            pltpu.VMEM((OUT_PARTS, rows * STEPS, out_cols), bf16),
            pltpu.VMEM((OUT_PARTS, rows * STEPS, out_cols), bf16),
            dma((chunks,)),
            dma((2,)),
            dma((OUT_PARTS,)),
            dma((chunks,)),
            dma((chunks,)),
            dma((n // 2,)),
            dma((n // 2,)),
            dma((n,)),
            dma((n,)),
            dma,
            dma,
            dma((2 * n,)),
            dma((2 * n,)),
            dma((OUT_PARTS,)),
            dma((OUT_PARTS,)),
        ],
        compiler_params=pltpu.CompilerParams(
            collective_id=0, has_side_effects=True, vmem_limit_bytes=56 * 2**20
        ),
    )(
        hidden,
        norm_gain[None, :],
        lengths,
        positions,
        query_weight,
        key_matrix,
        value_matrix,
        output_weight,
        key_cache_rows.reshape(slots, cache_cols),
        value_cache_rows.reshape(slots, cache_cols),
    )
    out, new_k, new_v = pl.pallas_call(
        hand_over,
        out_shape=(
            jax.ShapeDtypeStruct(out.shape, bf16),
            jax.ShapeDtypeStruct(new_k.shape, bf16),
            jax.ShapeDtypeStruct(new_v.shape, bf16),
        ),
        in_specs=[vmem] * 3,
        out_specs=(vmem,) * 3,
    )(out, new_k, new_v)
    return (out, new_k[:, None, :], new_v[:, None, :])


def solution(mesh):
    in_specs = (
        P(None, "rep", "gx"),
        P("gx"),
        P("gx", "yz"),
        P("gx", "yz"),
        P("gx", "yz"),
        P("yz", "gx"),
        P(("rep", "gx", "yz"), None, None),
        P(("rep", "gx", "yz"), None, None),
        P(("rep", "gx", "yz")),
        P("rep"),
    )
    out_specs = (
        P(None, "rep", "gx"),
        P(None, ("rep", "gx", "yz"), None),
        P(None, ("rep", "gx", "yz"), None),
    )
    return jax.shard_map(
        per_device, mesh=mesh, in_specs=in_specs, out_specs=out_specs, check_vma=False
    )
```
